32 devices in a mesh: col: 8 (over z, x), row: 4 (over y, core).
Axes of the slice: x: 2, y: 2, z: 4, core: 2. Of those that a mesh axis runs over, the one named last changes fastest.
Arguments:
- object_field: float32 [2, 1024, 8192], P(None, 'row', 'col'), may hold values from -6 to 6
- probe_wave: float32 [2, 256, 256], replicated, may hold values from -6 to 6
- amplitude: bfloat16 [512, 256, 256], P(('col', 'row')), may hold values from 0.5 to 4
- owners: int32 [512, 1], P(('col', 'row')), may hold values from 0 to 7; in each aligned block of 16 rows (0 to 15, 16 to 31, ...) at most 4 rows name the same one
- row_offset: int32 [512], P(('col', 'row')), may hold values from 0 to 255
- col_offset: int32 [512], P(('col', 'row')), may hold values from 0 to 1023
Outputs:
- new_object: float32 [2, 1024, 8192], P(None, 'row', 'col')
- probe_gradient: float32 [2, 256, 256], replicated
The draws below stay inside these ranges and needn't reach their ends.
Inputs may be any that keep to these rules, and one draw needn't show every extreme that they name: `owners`: within the 16 frames of one device no owner is named more than 4 times, a bound that some block reaches.
All inputs are finite; a program needn't handle non-finite values.
Results may differ from the reference program's by a relative error of at most 0.0003.
Values may be sent and summed in bfloat16 or wider, within the bound.
No kernel may reach another device: no remote copies, remote signals or barrier semaphores. Data moves between devices by JAX's collectives and lax.ppermute only.
A program may use at most 128 MiB of HBM per device.

```python
import math
import jax
import jax.numpy as jnp
import numpy as np
from jax import lax

FRAME = 256
TH = 256
TW = 1024
ACQ = 16
CAP = 4
FRAMES = 512
HEIGHT = 1024
WIDTH = 8192
N_COL = 8
N_ROW = 4


def place_ends(result, own_key, smallest, largest):
    longest = result.shape.index(max(result.shape))
    spots = []
    for shift in (0, 1):
        where = [jax.random.randint(jax.random.fold_in(own_key, axis), (), 0, length) for axis, length in enumerate(result.shape)]
        where[longest] = (where[longest] + shift) % result.shape[longest]
        spots.append(tuple(where))
    return result.at[spots[0]].set(smallest).at[spots[1]].set(largest)


def steps_of(own_key, extent, cuts, least, largest):
    def one(axis_at, blocks):
        heights = jax.random.uniform(jax.random.fold_in(jax.random.fold_in(own_key, 6), axis_at), (blocks,), jnp.float32, least / len(cuts), largest / len(cuts))
        return jnp.repeat(jnp.exp(heights), extent[axis_at] // blocks).reshape((-1,) + (1,) * (len(extent) - axis_at - 1))

    gain = one(*cuts[0])
    for cut in cuts[1:]:
        gain = gain * one(*cut)
    return gain


def deal_out(key, own, number, rows, number_of, top, most, lean):
    ranking = jax.random.permutation(key, number_of)
    packed, usual = load_shares(number_of, rows * top, most, lean, True), load_shares(number_of, rows * top, most, lean, False)
    places = jnp.arange(number_of)

    def named(sizes, turn):
        used = int((sizes > 0).sum())
        fixed = max(1, used // 4)
        moved = fixed + (places - fixed + turn * (used - fixed)) % max(1, number_of - fixed)
        return jnp.zeros((number_of,), jnp.int32).at[ranking[jnp.where(places < fixed, places, moved)]].set(jnp.asarray(sizes, jnp.int32))

    sizes = jnp.where(number % 4 == 0, named(packed, number // 4), named(usual, number - number // 4 - 1))
    mixed = jax.random.permutation(jax.random.fold_in(own, 3), number_of)
    donor, taker = mixed[0:number_of // 2 * 2:2], mixed[1:number_of // 2 * 2:2]
    room = jnp.minimum(sizes[donor] - 1, most - sizes[taker]) // 2
    room = jnp.where((donor == ranking[0]) | (taker == ranking[0]) | (sizes[taker] == 0), 0, jnp.maximum(room, 0))
    moved = jax.random.randint(jax.random.fold_in(own, 4), (number_of // 2,), 0, 1 << 20) % (room + 1)
    sizes = sizes.at[donor].add(-moved).at[taker].add(moved)
    items = jnp.searchsorted(jnp.cumsum(sizes), jnp.arange(rows * top), side="right").astype(jnp.int32)
    grid = items.reshape(top, rows).T
    grid = grid[jax.random.permutation(jax.random.fold_in(own, 1), rows)]
    turn = jax.random.randint(jax.random.fold_in(own, 2), (rows, 1), 0, top)
    return jnp.take_along_axis(grid, (jnp.arange(top)[None, :] + turn) % top, axis=1)


def load_shares(count, total, bound, skew, full):
    weights = [(1 << 20) // math.isqrt(rank ** skew) + 1 for rank in range(1, count + 1)]
    largest = bound if full else min(bound, max(-(-total // count), total * weights[0] // sum(weights)))
    least = 1 if total - largest >= count - 1 else 0
    counts, rest = [largest] + [least] * (count - 1), total - largest - least * (count - 1)
    while rest > 0:
        candidates = [i for i in range(1, count) if counts[i] < largest] or [i for i in range(1, count) if counts[i] < bound]
        whole, remaining = sum([weights[i] for i in candidates]), rest
        for i in candidates:
            more = min(bound - counts[i], max(1, remaining * weights[i] // whole), rest)
            counts[i] = counts[i] + more
            rest = rest - more
    return np.array(counts)


def noise(own_key, dims, spread, most, shards=(), kind=jnp.bfloat16):
    entries = jax.random.normal(own_key, dims, jnp.float32) * spread
    if len(shards) > 0:
        entries = steps_of(own_key, dims, shards, -0.22, 0.18) * entries
    return jnp.clip(entries, min=-most, max=most).astype(kind)


def setup_inputs(seed: int = 0) -> dict:
    key_list = jax.random.split(jax.random.key(seed), 7)
    object_field = noise(key_list[0], (2, HEIGHT, WIDTH), 1.0, 6.0, ((1, 4), (2, 8)), jnp.float32)
    probe_wave = noise(key_list[1], (2, FRAME, FRAME), 1.0, 6.0, (), jnp.float32)
    amplitude = jnp.clip(jnp.exp(math.log(4.0) - 2.0794415 * jax.random.uniform(key_list[2], (FRAMES, FRAME, FRAME), jnp.float32) ** steps_of(key_list[2], (FRAMES, FRAME, FRAME), ((0, 32),), -0.2, 0.2)), 0.5, 4.0).astype(jnp.bfloat16)
    owners_keys = jax.random.split(jax.random.fold_in(key_list[3], 1), FRAMES // ACQ)
    owners_turns = jax.random.permutation(jax.random.fold_in(key_list[3], 3), FRAMES // ACQ)
    owners = jax.vmap(lambda own, number: deal_out(jax.random.fold_in(key_list[3], 2), own, number, ACQ, N_COL, 1, CAP, 2))(owners_keys, owners_turns).reshape((FRAMES, 1))
    row_offset = place_ends(jax.random.randint(key_list[4], (FRAMES,), 0, TH), jax.random.fold_in(key_list[4], 1), 0, TH - 1).astype(jnp.int32)
    col_offset = place_ends(jax.random.randint(key_list[5], (FRAMES,), 0, TW), jax.random.fold_in(key_list[5], 1), 0, TW - 1).astype(jnp.int32)
    return dict(object_field=object_field, probe_wave=probe_wave, amplitude=amplitude, owners=owners, row_offset=row_offset, col_offset=col_offset)


HIGHEST = lax.Precision.HIGHEST
step_size = 0.05
smooth_weight = 0.5

def fourier_tables(length):
    indices = jnp.arange(length, dtype=jnp.int32)
    product = indices[:, None] * indices[None, :] % length
    angles = product.astype(jnp.float32) * (2.0 * math.pi / length)
    factor = 1.0 / math.sqrt(length)
    return (jnp.cos(angles) * factor, jnp.sin(angles) * factor)

def sandwich(x_real, x_imag, mat_real, mat_imag):
    mid_real = jnp.einsum('jk,bkl->bjl', mat_real, x_real, precision=HIGHEST) - jnp.einsum('jk,bkl->bjl', mat_imag, x_imag, precision=HIGHEST)
    mid_imag = jnp.einsum('jk,bkl->bjl', mat_real, x_imag, precision=HIGHEST) + jnp.einsum('jk,bkl->bjl', mat_imag, x_real, precision=HIGHEST)
    out_real = jnp.einsum('bjk,kl->bjl', mid_real, mat_real, precision=HIGHEST) - jnp.einsum('bjk,kl->bjl', mid_imag, mat_imag, precision=HIGHEST)
    out_imag = jnp.einsum('bjk,kl->bjl', mid_real, mat_imag, precision=HIGHEST) + jnp.einsum('bjk,kl->bjl', mid_imag, mat_real, precision=HIGHEST)
    return (out_real, out_imag)

def frame_residual(patch_real, patch_imag, probe_wave, measured, cosines, sines):
    exit_real = probe_wave[0] * patch_real - probe_wave[1] * patch_imag
    exit_imag = probe_wave[0] * patch_imag + probe_wave[1] * patch_real
    far_real, far_imag = sandwich(exit_real, exit_imag, cosines, -sines)
    magnitude = jnp.sqrt(far_real * far_real + far_imag * far_imag)
    scaling = measured.astype(jnp.float32) / jnp.maximum(magnitude, 1.0)
    back_real, back_imag = sandwich(scaling * far_real, scaling * far_imag, cosines, sines)
    return (exit_real - back_real, exit_imag - back_imag)

def reference(object_field, probe_wave, amplitude, owners, row_offset, col_offset):
    cosines, sines = fourier_tables(FRAME)
    half_frame = FRAME // 2
    padded = jnp.pad(object_field, ((0, 0), (half_frame, half_frame), (half_frame, half_frame)))
    frame_ids = jnp.arange(FRAMES, dtype=jnp.int32)
    strip_ids = frame_ids // ACQ % N_ROW
    top_rows = (strip_ids * TH + row_offset).astype(jnp.int32)
    left_cols = (owners[:, 0] * TW + col_offset).astype(jnp.int32)
    block_count = FRAMES // ACQ
    anchor = jnp.zeros((), jnp.int32)

    def one_block(state_pair, inputs):
        grad_now, probe_now = state_pair
        measured, block_tops, block_lefts = inputs

        def take_patch(top_row, left_col):
            return lax.dynamic_slice(padded, (anchor, top_row, left_col), (2, FRAME, FRAME))
        patches = jax.vmap(take_patch)(block_tops, block_lefts)
        wave_real, wave_imag = frame_residual(patches[:, 0], patches[:, 1], probe_wave, measured, cosines, sines)
        probe_now = probe_now + jnp.stack([lax.optimization_barrier(jnp.sum(patches[:, 0] * wave_real + patches[:, 1] * wave_imag, axis=0)), lax.optimization_barrier(jnp.sum(patches[:, 0] * wave_imag - patches[:, 1] * wave_real, axis=0))])
        obj_real = probe_wave[0] * wave_real + probe_wave[1] * wave_imag
        obj_imag = probe_wave[0] * wave_imag - probe_wave[1] * wave_real

        def add_one(number, running):
            addend = jnp.stack([obj_real[number], obj_imag[number]])
            current = lax.dynamic_slice(running, (anchor, block_tops[number], block_lefts[number]), (2, FRAME, FRAME))
            return lax.dynamic_update_slice(running, current + addend, (anchor, block_tops[number], block_lefts[number]))
        grad_now = lax.fori_loop(0, ACQ, add_one, grad_now)
        return ((grad_now, probe_now), None)
    inputs = (amplitude.reshape(block_count, ACQ, FRAME, FRAME), top_rows.reshape(block_count, ACQ), left_cols.reshape(block_count, ACQ))
    start = (jnp.zeros(padded.shape, jnp.float32), jnp.zeros((2, FRAME, FRAME), jnp.float32))
    (grad_full, probe_total), unused = lax.scan(one_block, start, inputs)
    data_grad = grad_full[:, half_frame:half_frame + HEIGHT, half_frame:half_frame + WIDTH]
    edged = jnp.pad(object_field, ((0, 0), (1, 1), (1, 1)))
    laplacian = 4.0 * object_field - edged[:, :-2, 1:-1] - edged[:, 2:, 1:-1] - edged[:, 1:-1, :-2] - edged[:, 1:-1, 2:]
    new_object = object_field - step_size * (data_grad + smooth_weight * laplacian)
    probe_gradient = probe_total / math.sqrt(FRAMES)
    return (new_object, probe_gradient)
```

```python
import math

import jax
import jax.numpy as jnp
import numpy as np
from jax import lax
from jax.sharding import PartitionSpec as P
from jax.experimental import pallas as pl
from jax.experimental.pallas import tpu as pltpu


def transform_tables(length):
    half = length // 2
    n = np.arange(half)

    def table(k):
        angles = (n[:, None] * k[None, :]) % length * (2.0 * np.pi / length)
        c, s = np.cos(angles) / np.sqrt(length), np.sin(angles) / np.sqrt(length)
        return np.block([[c, -s], [s, c]]).astype(np.float32)

    def parts(m):
        high = m.astype(jnp.bfloat16)
        return high, (m - high.astype(np.float32)).astype(jnp.bfloat16)

    even, odd = table(2 * n), table(2 * n + 1)
    rights = [np.concatenate([h, h, l], 0) for h, l in map(parts, (even, odd, even.T, odd.T))]
    lefts = [np.concatenate([h, h, l], 1) for h, l in map(parts, (even.T, odd.T, even, odd))]
    pick = np.eye(length, dtype=np.float32)[np.concatenate([2 * n, 2 * n + 1])].astype(jnp.bfloat16)
    return jnp.asarray(np.stack(rights)), jnp.asarray(np.stack(lefts)), jnp.asarray(np.stack([pick, pick.T]))


def dot(a, b):
    return jnp.dot(a, b, preferred_element_type=jnp.float32)


def cat(parts, axis):
    return jnp.concatenate(parts, axis=axis)


def put(ref, where, x, rows, cols):
    high = x.astype(jnp.bfloat16)
    ref[where, 0, rows, cols] = high
    ref[where, 1, rows, cols] = (x - high.astype(jnp.float32)).astype(jnp.bfloat16)


def dot_right(ref, where, table):
    high = ref[where, 0]
    return dot(cat([high, ref[where, 1], high], 1), table)


def dot_left(table, ref, where):
    high = ref[where, 0]
    return dot(table, cat([high, ref[where, 1], high], 0))


CH = 16
PAIR = 2
step_size = 0.05
smooth_weight = 0.5


def frames_step(places, slots, keep_all, frames_ref, ext_ref, right_ref, left_ref, pick_ref, grad_ref, probe_ref, gp_ref, wave_ref, prolled_ref, one_ref, two_ref, three_ref, four_ref):
    f = wave_ref.shape[2]
    h = f // 2
    count = len(places)
    each = range(count)
    halves = (slice(0, h), slice(h, f))
    lane = lax.broadcasted_iota(jnp.int32, (CH, h), 1)
    sub = lax.broadcasted_iota(jnp.int32, (8, f + h), 0)
    rr = [lax.rem(r, 8) for r, c in places]
    cc = [lax.rem(c, 128) for r, c in places]
    r8 = [pl.multiple_of(places[n][0] - rr[n], 8) for n in each]
    window = [pl.ds(pl.multiple_of(places[n][1] - cc[n], 128), f + h) for n in each]
    keep = [lane >= cc[n] for n in each]
    keep_rows = [sub >= rr[n] for n in each]

    def patch(n, p, i):
        w = ext_ref[p, pl.ds(pl.multiple_of(r8[n] + i, 8), CH), window[n]]
        if i == 0:
            w2 = ext_ref[p, pl.ds(pl.multiple_of(r8[n] + f, 8), 8), window[n]]
            w = cat([jnp.where(keep_rows[n], w[:8], w2), w[8:]], 0)
        return jnp.where(keep[n], w[:, :h], w[:, f:]), w[:, h:f]

    def probe(n, p, i):
        rows = pl.ds(8 - rr[n] + i, CH)
        y0 = pltpu.roll(probe_ref[p, 0, rows, :], cc[n], 1)
        y1 = pltpu.roll(probe_ref[p, 1, rows, :], cc[n], 1)
        return jnp.where(keep[n], y0, y1), jnp.where(keep[n], y1, y0)

    for n in each:
        for i in range(0, f, CH):
            rows = slice(i, i + CH)
            qr, qi, pr, pi = patch(n, 0, i), patch(n, 1, i), probe(n, 0, i), probe(n, 1, i)
            er, ei = [], []
            for t in range(2):
                prolled_ref[n, 0, rows, halves[t]] = pr[t]
                prolled_ref[n, 1, rows, halves[t]] = pi[t]
                er.append(pr[t] * qr[t] - pi[t] * qi[t])
                ei.append(pr[t] * qi[t] + pi[t] * qr[t])
                wave_ref[n, 0, rows, halves[t]] = er[t]
                wave_ref[n, 1, rows, halves[t]] = ei[t]
            put(one_ref.at[n], 0, er[0] + er[1], rows, halves[0])
            put(one_ref.at[n], 0, ei[0] + ei[1], rows, halves[1])
            put(one_ref.at[n], 1, er[0] - er[1], rows, halves[0])
            put(one_ref.at[n], 1, ei[0] - ei[1], rows, halves[1])
    for n in each:
        for w in range(2):
            y = dot_right(one_ref.at[n], w, right_ref[w])
            for i in range(0, h, CH):
                a, b = y[i:i + CH], y[h + i:h + i + CH]
                u, v = a + b, a - b
                put(two_ref.at[n], 0, u[:, :h], slice(i, i + CH), halves[w])
                put(two_ref.at[n], 0, u[:, h:], slice(h + i, h + i + CH), halves[w])
                put(two_ref.at[n], 1, v[:, :h], slice(i, i + CH), halves[w])
                put(two_ref.at[n], 1, v[:, h:], slice(h + i, h + i + CH), halves[w])
    for n in each:
        meas = dot(pick_ref[0], dot(frames_ref[slots[n]], pick_ref[1]).astype(jnp.bfloat16))
        for w in range(2):
            far = dot_left(left_ref[w], two_ref.at[n], w)
            for i in range(0, h, CH):
                xr, xi = far[i:i + CH], far[h + i:h + i + CH]
                s = meas[w * h + i:w * h + i + CH] * lax.rsqrt(jnp.maximum(xr * xr + xi * xi, 1.0))
                put(three_ref.at[n], w, xr * s, slice(i, i + CH), slice(0, f))
                put(three_ref.at[n], w, xi * s, slice(h + i, h + i + CH), slice(0, f))
    for n in each:
        be, bo = dot_left(left_ref[2], three_ref.at[n], 0), dot_left(left_ref[3], three_ref.at[n], 1)
        for i in range(0, h, CH):
            for part in range(2):
                j = part * h + i
                top, bot = be[j:j + CH] + bo[j:j + CH], be[j:j + CH] - bo[j:j + CH]
                for w in range(2):
                    put(four_ref.at[n], w, top[:, halves[w]], slice(i, i + CH), halves[part])
                    put(four_ref.at[n], w, bot[:, halves[w]], slice(h + i, h + i + CH), halves[part])
    for n in each:
        de, do = dot_right(four_ref.at[n], 0, right_ref[2]), dot_right(four_ref.at[n], 1, right_ref[3])
        fits = lane < 128 - cc[n]
        for i in range(0, f, CH):
            rows = slice(i, i + CH)
            a, b = de[rows], do[rows]
            lf, rt = a + b, a - b
            qr, qi = patch(n, 0, i), patch(n, 1, i)
            outs, back = [[], []], [[], []]
            for t, x in enumerate((lf, rt)):
                dr = wave_ref[n, 0, rows, halves[t]] - x[:, :h]
                di = wave_ref[n, 1, rows, halves[t]] - x[:, h:]
                if n:
                    dr, di = jnp.where(keep_all, dr, 0.0), jnp.where(keep_all, di, 0.0)
                pr, pi = prolled_ref[n, 0, rows, halves[t]], prolled_ref[n, 1, rows, halves[t]]
                outs[0].append(pr * dr + pi * di)
                outs[1].append(pr * di - pi * dr)
                back[0].append(qr[t] * dr + qi[t] * di)
                back[1].append(qr[t] * di - qi[t] * dr)
            for p in range(2):
                first = jnp.where(keep[n], outs[p][0], 0.0)
                full = cat([first, outs[p][1], outs[p][0] - first], 1)
                if i == 0:
                    head = jnp.where(keep_rows[n], full[:8], 0.0)
                    grad_ref[p, pl.ds(pl.multiple_of(r8[n] + f, 8), 8), window[n]] += full[:8] - head
                    full = cat([head, full[8:]], 0)
                grad_ref[p, pl.ds(pl.multiple_of(r8[n] + i, 8), CH), window[n]] += full
                y0 = pltpu.roll(back[p][0], lax.rem(128 - cc[n], 128), 1)
                y1 = pltpu.roll(back[p][1], lax.rem(128 - cc[n], 128), 1)
                spot = pl.ds(8 - rr[n] + i, CH)
                gp_ref[p, 0, spot, :] += jnp.where(fits, y0, y1)
                gp_ref[p, 1, spot, :] += jnp.where(fits, y1, y0)


def kernel(info_ref, frames_ref, ext_ref, probe_in, right_ref, left_ref, pick_ref, grad_ref, gp_out, list_ref, probe_ref, gp_ref, *scratch):
    f = probe_in.shape[1]
    h = f // 2
    grad_ref[...] = jnp.zeros_like(grad_ref)
    gp_ref[...] = jnp.zeros_like(gp_ref)
    for p in range(2):
        for t in range(2):
            cols = slice(t * h, t * h + h)
            probe_ref[p, t, 0:8, :] = probe_in[p, f - 8:f, cols]
            probe_ref[p, t, 8:8 + f, :] = probe_in[p, :, cols]
    def note(slot, total):
        @pl.when(info_ref[slot, 2] > 0)
        def _():
            list_ref[total] = slot

        return total + info_ref[slot, 2]

    total = lax.fori_loop(0, frames_ref.shape[0], note, 0)

    @pl.loop(0, (total + PAIR - 1) // PAIR)
    def _(k):
        slots = [list_ref[jnp.minimum(k * PAIR + n, total - 1)] for n in range(PAIR)]
        places = [(info_ref[n, 0], info_ref[n, 1]) for n in slots]
        frames_step(places, slots, k * PAIR + 1 < total, frames_ref, ext_ref, right_ref, left_ref, pick_ref, grad_ref, probe_ref, gp_ref, *scratch)

    for p in range(2):
        for t in range(2):
            cols = slice(t * h, t * h + h)
            gp_out[p, 0:f - 8, cols] = gp_ref[p, t, 8:f, :]
            gp_out[p, f - 8:f, cols] = gp_ref[p, t, f:f + 8, :] + gp_ref[p, t, 0:8, :]


def run_frames(info, frames, ext, probe, tables):
    vm = pl.BlockSpec(memory_space=pltpu.VMEM)
    f = probe.shape[1]
    split = pltpu.VMEM((PAIR, 2, 2, f, f), jnp.bfloat16)
    return pl.pallas_call(
        kernel,
        out_shape=(jax.ShapeDtypeStruct(ext.shape, jnp.float32), jax.ShapeDtypeStruct(probe.shape, jnp.float32)),
        in_specs=[pl.BlockSpec(memory_space=pltpu.SMEM)] + [vm] * 6,
        out_specs=(vm, vm),
        scratch_shapes=[pltpu.SMEM((info.shape[0],), jnp.int32)] + [pltpu.VMEM((2, 2, f + 8, f // 2), jnp.float32)] * 2 + [pltpu.VMEM((PAIR, 2, f, f), jnp.float32)] * 2 + [split] * 4,
        compiler_params=pltpu.CompilerParams(vmem_limit_bytes=60 << 20),
    )(info, frames, ext, probe, *tables)


def padded(shard, sides, width):
    for axis, dim in sides:
        count, length = (lax.axis_size(axis), shard.shape[dim])
        up = [(i, (i + 1) % count) for i in range(count - 1)]
        down = [(j, i) for i, j in up]
        last = lax.slice_in_dim(shard, length - width, length, axis=dim)
        leading = lax.slice_in_dim(shard, 0, width, axis=dim)
        before = lax.ppermute(last, axis, up)
        after = lax.ppermute(leading, axis, down)
        shard = jnp.concatenate([before, shard, after], axis=dim)
    return shard


def shifted(block, axis, distance):
    devices = range(lax.axis_size(axis))
    route = [(i - distance, i) for i in devices if i - distance in devices]
    return lax.ppermute(block, axis, route)


def summed(part, axes):
    count = lax.axis_size(axes)
    pieces = part.reshape(count, -1, part.shape[-1])
    piece = jnp.sum(lax.all_to_all(pieces, axes, 0, 0, tiled=True), axis=0)
    whole = lax.all_to_all(jnp.broadcast_to(piece[None], pieces.shape), axes, 0, 0, tiled=True)
    return whole.reshape(part.shape)


def on_device(object_field, probe_wave, amplitude, owners, row_offset, col_offset):
    tile_height = object_field.shape[1]
    tile_width = object_field.shape[2]
    frame_size = probe_wave.shape[1]
    half_frame = frame_size // 2
    acquired = amplitude.shape[0]
    col_count = lax.axis_size("col")
    extended = padded(object_field, (("col", 2), ("row", 1)), half_frame)
    capacity = 2 * acquired // col_count
    slot_count = col_count * capacity
    frame_ids = jnp.arange(acquired, dtype=jnp.int32)
    target = owners[:, 0]
    earlier = (target[:, None] == target[None, :]) & (frame_ids[None, :] < frame_ids[:, None])
    slot_rank = jnp.sum(earlier.astype(jnp.int32), axis=1)
    slot_ids = target * capacity + slot_rank
    chooser = (jnp.arange(slot_count, dtype=jnp.int32)[:, None] == slot_ids[None, :]).astype(
        jnp.int32
    )
    source_ids = jnp.sum(chooser * frame_ids[None, :], axis=1)
    filled = jnp.sum(chooser, axis=1)
    packed = jnp.take(amplitude, source_ids, axis=0) * filled.astype(jnp.bfloat16)[:, None, None]
    frame_info = jnp.stack(
        [jnp.take(row_offset, source_ids), jnp.take(col_offset, source_ids), filled], axis=1
    )
    got_frames, got_info = (
        lax.all_to_all(
            packed.reshape(col_count, capacity, frame_size, frame_size),
            "col",
            split_axis=0,
            concat_axis=0,
            tiled=True,
        ),
        lax.all_to_all(
            frame_info.reshape(col_count, capacity, 3),
            "col",
            split_axis=0,
            concat_axis=0,
            tiled=True,
        ),
    )
    got_frames = got_frames.reshape(slot_count, frame_size, frame_size)
    got_info = got_info.reshape(slot_count, 3)

    grad_ext, probe_part = run_frames(
        got_info, got_frames, extended, probe_wave, transform_tables(frame_size)
    )
    from_right = shifted(grad_ext[:, :, :half_frame], "col", -1)
    from_left = shifted(grad_ext[:, :, tile_width + half_frame :], "col", 1)
    middle = grad_ext[:, :, half_frame : half_frame + tile_width]
    middle = middle.at[:, :, tile_width - half_frame :].add(from_right)
    middle = middle.at[:, :, :half_frame].add(from_left)
    from_below = shifted(middle[:, :half_frame], "row", -1)
    from_above = shifted(middle[:, tile_height + half_frame :], "row", 1)
    data_grad = middle[:, half_frame : half_frame + tile_height]
    data_grad = data_grad.at[:, tile_height - half_frame :].add(from_below)
    data_grad = data_grad.at[:, :half_frame].add(from_above)
    upper = extended[
        :, half_frame - 1 : half_frame - 1 + tile_height, half_frame : half_frame + tile_width
    ]
    lower = extended[
        :, half_frame + 1 : half_frame + 1 + tile_height, half_frame : half_frame + tile_width
    ]
    western = extended[
        :, half_frame : half_frame + tile_height, half_frame - 1 : half_frame - 1 + tile_width
    ]
    eastern = extended[
        :, half_frame : half_frame + tile_height, half_frame + 1 : half_frame + 1 + tile_width
    ]
    laplacian = 4.0 * object_field - upper - lower - western - eastern
    new_object = object_field - step_size * (data_grad + smooth_weight * laplacian)
    probe_total = summed(probe_part, ("col", "row"))
    frames_total = acquired * col_count * lax.axis_size("row")
    probe_gradient = probe_total / math.sqrt(frames_total)
    return (new_object, probe_gradient)


def solution(mesh):
    in_specs = (
        P(None, "row", "col"),
        P(),
        P(("col", "row"), None, None),
        P(("col", "row"), None),
        P(("col", "row")),
        P(("col", "row")),
    )
    out_specs = (P(None, "row", "col"), P())
    return jax.shard_map(
        on_device, mesh=mesh, in_specs=in_specs, out_specs=out_specs, check_vma=False
    )
```

```python
import math

import jax
import jax.numpy as jnp
import numpy as np
from jax import lax
from jax.sharding import PartitionSpec as P
from jax.experimental import pallas as pl
from jax.experimental.pallas import tpu as pltpu


def transform_tables(length):
    half = length // 2
    n = np.arange(half)

    def table(k):
        angles = (n[:, None] * k[None, :]) % length * (2.0 * np.pi / length)
        c, s = np.cos(angles) / np.sqrt(length), np.sin(angles) / np.sqrt(length)
        return np.block([[c, -s], [s, c]]).astype(np.float32)

    def parts(m):
        high = m.astype(jnp.bfloat16)
        return high, (m - high.astype(np.float32)).astype(jnp.bfloat16)

    even, odd = table(2 * n), table(2 * n + 1)
    rights = [np.concatenate([h, l], 0) for h, l in map(parts, (even, odd, even.T, odd.T))]
    lefts = [np.concatenate([h, l], 1) for h, l in map(parts, (even.T, odd.T, even, odd))]
    pick = np.eye(length, dtype=np.float32)[np.concatenate([2 * n, 2 * n + 1])].astype(jnp.bfloat16)
    return jnp.asarray(np.stack(rights)), jnp.asarray(np.stack(lefts)), jnp.asarray(np.stack([pick, pick.T]))


def dot(a, b):
    return jnp.dot(a, b, preferred_element_type=jnp.float32)


def cat(parts, axis):
    return jnp.concatenate(parts, axis=axis)


def put(ref, where, x, rows, cols):
    high = x.astype(jnp.bfloat16)
    ref[where, 0, rows, cols] = high
    ref[where, 1, rows, cols] = (x - high.astype(jnp.float32)).astype(jnp.bfloat16)


def dot_right(ref, where, table):
    size = table.shape[1]
    high = ref[where, 0]
    return dot(cat([high, ref[where, 1], high], 1), cat([table[:size], table], 0))


def dot_left(table, ref, where):
    size = table.shape[0]
    high = ref[where, 0]
    return dot(cat([table[:, :size], table], 1), cat([high, ref[where, 1], high], 0))


CH = 16
PAIR = 4
step_size = 0.05
smooth_weight = 0.5
BASE = 2


def frames_step(places, slots, keep_all, frames_ref, ext_ref, right_ref, left_ref, pick_ref, grad_ref, probe_ref, gp_ref, wave_ref, prolled_ref, one_ref, two_ref, three_ref, four_ref):
    f = wave_ref.shape[2]
    h = f // 2
    count = len(places)
    each = range(count)
    halves = (slice(0, h), slice(h, f))
    lane = lax.broadcasted_iota(jnp.int32, (CH, h), 1)
    sub = lax.broadcasted_iota(jnp.int32, (8, f + h), 0)
    rr = [lax.rem(r, 8) for r, c in places]
    cc = [lax.rem(c, 128) for r, c in places]
    r8 = [pl.multiple_of(places[n][0] - rr[n], 8) for n in each]
    window = [pl.ds(pl.multiple_of(places[n][1] - cc[n], 128), f + h) for n in each]
    keep = [lane >= cc[n] for n in each]
    keep_rows = [sub >= rr[n] for n in each]

    def patch(n, p, i):
        w = ext_ref[p, pl.ds(pl.multiple_of(r8[n] + i, 8), CH), window[n]]
        if i == 0:
            w2 = ext_ref[p, pl.ds(pl.multiple_of(r8[n] + f, 8), 8), window[n]]
            w = cat([jnp.where(keep_rows[n], w[:8], w2), w[8:]], 0)
        return jnp.where(keep[n], w[:, :h], w[:, f:]), w[:, h:f]

    def probe(n, p, i):
        rows = pl.ds(8 - rr[n] + i, CH)
        y0 = pltpu.roll(probe_ref[p, 0, rows, :], cc[n], 1)
        y1 = pltpu.roll(probe_ref[p, 1, rows, :], cc[n], 1)
        return jnp.where(keep[n], y0, y1), jnp.where(keep[n], y1, y0)

    for n in each:
        for i in range(0, f, CH):
            rows = slice(i, i + CH)
            qr, qi, pr, pi = patch(n, 0, i), patch(n, 1, i), probe(n, 0, i), probe(n, 1, i)
            er, ei = [], []
            for t in range(2):
                prolled_ref[n, 0, rows, halves[t]] = pr[t]
                prolled_ref[n, 1, rows, halves[t]] = pi[t]
                er.append(pr[t] * qr[t] - pi[t] * qi[t])
                ei.append(pr[t] * qi[t] + pi[t] * qr[t])
                wave_ref[n, 0, rows, halves[t]] = er[t]
                wave_ref[n, 1, rows, halves[t]] = ei[t]
            put(one_ref.at[n], 0, er[0] + er[1], rows, halves[0])
            put(one_ref.at[n], 0, ei[0] + ei[1], rows, halves[1])
            put(one_ref.at[n], 1, er[0] - er[1], rows, halves[0])
            put(one_ref.at[n], 1, ei[0] - ei[1], rows, halves[1])
    for n in each:
        for w in range(2):
            y = dot_right(one_ref.at[n], w, right_ref[w])
            for i in range(0, h, CH):
                a, b = y[i:i + CH], y[h + i:h + i + CH]
                u, v = a + b, a - b
                put(two_ref.at[n], 0, u[:, :h], slice(i, i + CH), halves[w])
                put(two_ref.at[n], 0, u[:, h:], slice(h + i, h + i + CH), halves[w])
                put(two_ref.at[n], 1, v[:, :h], slice(i, i + CH), halves[w])
                put(two_ref.at[n], 1, v[:, h:], slice(h + i, h + i + CH), halves[w])
    for n in each:
        meas = dot(pick_ref[0], dot(frames_ref[slots[n]], pick_ref[1]).astype(jnp.bfloat16))
        for w in range(2):
            far = dot_left(left_ref[w], two_ref.at[n], w)
            for i in range(0, h, CH):
                xr, xi = far[i:i + CH], far[h + i:h + i + CH]
                s = meas[w * h + i:w * h + i + CH] * lax.rsqrt(jnp.maximum(xr * xr + xi * xi, 1.0))
                put(three_ref.at[n], w, xr * s, slice(i, i + CH), slice(0, f))
                put(three_ref.at[n], w, xi * s, slice(h + i, h + i + CH), slice(0, f))
    for n in each:
        be, bo = dot_left(left_ref[2], three_ref.at[n], 0), dot_left(left_ref[3], three_ref.at[n], 1)
        for i in range(0, h, CH):
            for part in range(2):
                j = part * h + i
                top, bot = be[j:j + CH] + bo[j:j + CH], be[j:j + CH] - bo[j:j + CH]
                for w in range(2):
                    put(four_ref.at[n], w, top[:, halves[w]], slice(i, i + CH), halves[part])
                    put(four_ref.at[n], w, bot[:, halves[w]], slice(h + i, h + i + CH), halves[part])
    for n in each:
        de, do = dot_right(four_ref.at[n], 0, right_ref[2]), dot_right(four_ref.at[n], 1, right_ref[3])
        fits = lane < 128 - cc[n]
        for i in range(0, f, CH):
            rows = slice(i, i + CH)
            a, b = de[rows], do[rows]
            lf, rt = a + b, a - b
            qr, qi = patch(n, 0, i), patch(n, 1, i)
            outs, back = [[], []], [[], []]
            for t, x in enumerate((lf, rt)):
                dr = wave_ref[n, 0, rows, halves[t]] - x[:, :h]
                di = wave_ref[n, 1, rows, halves[t]] - x[:, h:]
                if n:
                    dr, di = jnp.where(keep_all[n], dr, 0.0), jnp.where(keep_all[n], di, 0.0)
                pr, pi = prolled_ref[n, 0, rows, halves[t]], prolled_ref[n, 1, rows, halves[t]]
                outs[0].append(pr * dr + pi * di)
                outs[1].append(pr * di - pi * dr)
                back[0].append(qr[t] * dr + qi[t] * di)
                back[1].append(qr[t] * di - qi[t] * dr)
            for p in range(2):
                first = jnp.where(keep[n], outs[p][0], 0.0)
                full = cat([first, outs[p][1], outs[p][0] - first], 1)
                if i == 0:
                    head = jnp.where(keep_rows[n], full[:8], 0.0)
                    grad_ref[p, pl.ds(pl.multiple_of(r8[n] + f, 8), 8), window[n]] += full[:8] - head
                    full = cat([head, full[8:]], 0)
                grad_ref[p, pl.ds(pl.multiple_of(r8[n] + i, 8), CH), window[n]] += full
                y0 = pltpu.roll(back[p][0], lax.rem(128 - cc[n], 128), 1)
                y1 = pltpu.roll(back[p][1], lax.rem(128 - cc[n], 128), 1)
                spot = pl.ds(8 - rr[n] + i, CH)
                gp_ref[p, 0, spot, :] += jnp.where(fits, y0, y1)
                gp_ref[p, 1, spot, :] += jnp.where(fits, y1, y0)


NOTE = 16


def pack_kernel(base, owners_ref, rows_ref, cols_ref, amp_ref, count_ref, *rest):
    main, rest = rest[:base], rest[base:]
    spare, (seen_ref, note_ref, sems) = rest[:-3], rest[-3:]
    acquired, f = amp_ref.shape[:2]
    col_count = main[0].shape[0]
    lane = lax.broadcasted_iota(jnp.int32, (NOTE, amp_ref.shape[2]), 1)
    line = lax.broadcasted_iota(jnp.int32, (NOTE, amp_ref.shape[2]), 0)
    note_ref[...] = jnp.zeros_like(note_ref)

    @pl.loop(0, col_count)
    def _(n):
        seen_ref[n] = 0

    def place(k, spared):
        owner = owners_ref[k, 0]
        rank = seen_ref[owner]
        seen_ref[owner] = rank + 1
        words = (owner + 1, rows_ref[k] // 256, lax.rem(rows_ref[k], 256), cols_ref[k] // 256, lax.rem(cols_ref[k], 256))
        note = jnp.zeros(lane.shape, jnp.int32)
        for n, word in enumerate(words):
            note = jnp.where((lane == n) & (line == 0), word, note)
        spot = jnp.where(rank < base, owner * base + rank, col_count * base + spared)
        note_ref[spot] = note.astype(jnp.float32).astype(jnp.bfloat16)

        for n in range(base):
            @pl.when(rank == n)
            def _():
                pltpu.make_async_copy(amp_ref.at[k], main[n].at[owner, pl.ds(0, f)], sems.at[k]).start()

        if spare:
            @pl.when(rank >= base)
            def _():
                pltpu.make_async_copy(amp_ref.at[k], spare[0].at[spared, pl.ds(0, f)], sems.at[k]).start()

        return spared + jnp.where(rank >= base, 1, 0)

    spared = lax.fori_loop(0, acquired, place, 0)
    count_ref[0] = spared
    copies = []
    for n in range(note_ref.shape[0]):
        slot = main[n % base].at[n // base] if n < col_count * base else spare[0].at[n - col_count * base]
        copies.append(pltpu.make_async_copy(note_ref.at[n], slot.at[pl.ds(f, NOTE)], sems.at[acquired + n]))
    for copy in copies:
        copy.start()

    @pl.loop(0, acquired)
    def _(k):
        pltpu.make_async_copy(amp_ref.at[k], main[0].at[0, pl.ds(0, f)], sems.at[k]).wait()

    for copy in copies:
        copy.wait()


def pack(owners, row_offset, col_offset, amplitude, base, col_count, spares):
    frame = (amplitude.shape[1] + NOTE, amplitude.shape[2])
    smem, hbm = pl.BlockSpec(memory_space=pltpu.SMEM), pl.BlockSpec(memory_space=pl.ANY)
    shapes = [jax.ShapeDtypeStruct((1,), jnp.int32)]
    shapes += [jax.ShapeDtypeStruct((col_count,) + frame, amplitude.dtype)] * base
    if spares:
        shapes.append(jax.ShapeDtypeStruct((spares,) + frame, amplitude.dtype))
    notes = col_count * base + spares
    return pl.pallas_call(
        lambda *refs: pack_kernel(base, *refs),
        out_shape=shapes,
        in_specs=[smem] * 3 + [pl.BlockSpec(memory_space=pltpu.VMEM)],
        out_specs=[smem] + [hbm] * (len(shapes) - 1),
        scratch_shapes=[
            pltpu.SMEM((col_count,), jnp.int32),
            pltpu.VMEM((notes, NOTE, frame[1]), amplitude.dtype),
            pltpu.SemaphoreType.DMA((amplitude.shape[0] + notes,)),
        ],
    )(owners, row_offset, col_offset, amplitude)


def own_terms_kernel(x_ref, west_ref, east_ref, north_ref, south_ref, out_ref):
    x = x_ref[0]
    height, width = x.shape
    row = lax.broadcasted_iota(jnp.int32, x.shape, 0)
    col = lax.broadcasted_iota(jnp.int32, x.shape, 1)
    h = west_ref.shape[2]
    cols = slice(h, h + width)
    above = jnp.where(row == 0, north_ref[0, h - 1:h, cols], pltpu.roll(x, 1, 0))
    below = jnp.where(row == height - 1, south_ref[0, 0:1, cols], pltpu.roll(x, height - 1, 0))
    before = jnp.where(col == 0, west_ref[0, :, h - 1:h], pltpu.roll(x, 1, 1))
    after = jnp.where(col == width - 1, east_ref[0, :, 0:1], pltpu.roll(x, width - 1, 1))
    laplacian = 4.0 * x - above - below - before - after
    out_ref[0] = x - (step_size * smooth_weight) * laplacian


def own_terms(field):
    blocks = [pl.BlockSpec((1,) + piece.shape[1:], lambda p: (p, 0, 0)) for piece in field]
    return pl.pallas_call(
        own_terms_kernel,
        grid=(2,),
        out_shape=jax.ShapeDtypeStruct(field[0].shape, jnp.float32),
        in_specs=blocks,
        out_specs=blocks[0],
        compiler_params=pltpu.CompilerParams(vmem_limit_bytes=60 << 20),
    )(*field)


def frames_kernel(layout, first, last, me_ref, *refs):
    refs = list(refs)
    take = lambda n: [refs.pop(0) for _ in range(n)]
    buffers = take(len(layout))
    pieces = take(5)
    constants = take(4)
    grads_in = take(0 if first else 2)
    outs = take(6 if last else 2)
    list_ref, note_ref, frames_ref, ext_ref, grad_ref, probe_ref, gp_ref, sems, frame_sems = take(9)
    probe_in, right_ref, left_ref, pick_ref = held = take(4)
    f = probe_in.shape[1]
    h = f // 2
    height, width = pieces[0].shape[1:]
    every = slice(None)
    areas = (
        (every, pl.ds(h, height), pl.ds(h, width)),
        (every, pl.ds(h, height), pl.ds(0, h)),
        (every, pl.ds(h, height), pl.ds(h + width, h)),
        (every, pl.ds(0, h)),
        (every, pl.ds(h + height, h)),
    )
    copies = [pltpu.make_async_copy(piece, ext_ref.at[area], sems.at[n]) for n, (piece, area) in enumerate(zip(pieces, areas))]
    late = [pltpu.make_async_copy(constants[n], held[n], sems.at[9 + n]) for n in range(4)]
    if not first:
        before_ref, before_gp_ref = take(2)
        carried = [
            pltpu.make_async_copy(grads_in[0], before_ref, sems.at[13]),
            pltpu.make_async_copy(grads_in[1], before_gp_ref, sems.at[14]),
        ]
    for copy in copies + late + ([] if first else carried):
        copy.start()
    scratch = refs
    notes = [
        pltpu.make_async_copy(
            buffers[b].at[pl.ds(0, len(slots)), pl.ds(f, NOTE)],
            note_ref.at[pl.ds(sum(len(x) for x in layout[:b]), len(slots))],
            sems.at[15 + b],
        )
        for b, slots in enumerate(layout)
    ]
    for copy in notes:
        copy.start()
    for copy in notes:
        copy.wait()
    lane = lax.broadcasted_iota(jnp.int32, (NOTE, note_ref.shape[2]), 1)
    row_scale = jnp.where(lane == 0, 65536.0, jnp.where(lane == 1, 256.0, jnp.where(lane == 2, 1.0, 0.0)))
    col_scale = jnp.where(lane == 3, 256.0, jnp.where(lane == 4, 1.0, 0.0))
    found = []
    for spot in range(note_ref.shape[0]):
        note = note_ref[spot].astype(jnp.float32)
        found.append((jnp.sum(note * row_scale).astype(jnp.int32), jnp.sum(note * col_scale).astype(jnp.int32)))
    total = 0
    for b, slots in enumerate(layout):
        for n, slot in enumerate(slots):
            spot = sum(len(x) for x in layout[:b]) + n
            row, col = found[spot]
            used = row // 65536 == me_ref[0] + 1

            @pl.when(used)
            def _():
                list_ref[total, 0] = lax.rem(row, 65536)
                list_ref[total, 1] = col
                list_ref[total, 2] = spot
                pltpu.make_async_copy(buffers[b].at[n, pl.ds(0, f)], frames_ref.at[spot], frame_sems.at[spot]).start()

            total = total + jnp.where(used, 1, 0)
    gp_ref[...] = jnp.zeros_like(gp_ref)
    grad_ref[...] = jnp.zeros_like(grad_ref)
    for copy in copies:
        copy.wait()
    for copy in late:
        copy.wait()
    for p in range(2):
        for t in range(2):
            cols = slice(t * h, t * h + h)
            probe_ref[p, t, 0:8, :] = probe_in[p, f - 8:f, cols]
            probe_ref[p, t, 8:8 + f, :] = probe_in[p, :, cols]

    @pl.loop(0, total)
    def _(k):
        spot = list_ref[k, 2]
        pltpu.make_async_copy(buffers[0].at[0, pl.ds(0, f)], frames_ref.at[spot], frame_sems.at[spot]).wait()

    @pl.loop(0, (total + PAIR - 1) // PAIR)
    def _(k):
        places, spots = [], []
        for n in range(PAIR):
            item = jnp.minimum(k * PAIR + n, total - 1)
            places.append((list_ref[item, 0], list_ref[item, 1]))
            spots.append(list_ref[item, 2])
        frames_step(places, spots, [k * PAIR + n < total for n in range(PAIR)], frames_ref, ext_ref, right_ref, left_ref, pick_ref, grad_ref, probe_ref, gp_ref, *scratch)

    if not first:
        for copy in carried:
            copy.wait()
        gp_ref[...] += before_gp_ref[...]

        @pl.loop(0, grad_ref.shape[1] // CH)
        def _(k):
            rows = pl.ds(pl.multiple_of(k * CH, CH), CH)
            grad_ref[:, rows, :] += before_ref[:, rows, :]

    if not last:
        ends = [(grad_ref, outs[0]), (gp_ref, outs[1])]
    else:
        spots = [
            (every, every, pl.ds(0, h)),
            (every, every, pl.ds(h + width, h)),
            (every, pl.ds(0, h), pl.ds(h, width)),
            (every, pl.ds(h + height, h), pl.ds(h, width)),
            areas[0],
        ]
        ends = [(grad_ref.at[spot], outs[n]) for n, spot in enumerate(spots)]
        for p in range(2):
            for t in range(2):
                cols = slice(t * h, t * h + h)
                outs[5][p, 0:f - 8, cols] = gp_ref[p, t, 8:f, :]
                outs[5][p, f - 8:f, cols] = gp_ref[p, t, f:f + 8, :] + gp_ref[p, t, 0:8, :]
    ends = [pltpu.make_async_copy(a, b, sems.at[n]) for n, (a, b) in enumerate(ends)]
    for copy in ends:
        copy.start()
    for copy in ends:
        copy.wait()


def run_frames(me, buffers, field, probe, tables, grads, last):
    layout = [list(range(buffer.shape[0])) for buffer in buffers]
    f = probe.shape[1]
    h = f // 2
    height, width = field[0].shape[1:]
    first = grads is None
    vm, hbm, smem = (pl.BlockSpec(memory_space=m) for m in (pltpu.VMEM, pl.ANY, pltpu.SMEM))
    f32 = jnp.float32
    ext, gp = (2, height + f, width + f), (2, 2, f + 8, h)
    if last:
        shapes = [(2, height + f, h)] * 2 + [(2, h, width)] * 2 + [(2, height, width), probe.shape]
        out_specs = [hbm] * 5 + [vm]
    else:
        shapes, out_specs = [ext, gp], [hbm] * 2
    spots = sum(len(x) for x in layout)
    split = pltpu.VMEM((PAIR, 2, 2, f, f), jnp.bfloat16)
    return pl.pallas_call(
        lambda *refs: frames_kernel(layout, first, last, *refs),
        out_shape=[jax.ShapeDtypeStruct(x, f32) for x in shapes],
        in_specs=[smem] + [hbm] * (len(buffers) + 9 + (0 if first else 2)),
        out_specs=out_specs,
        scratch_shapes=[pltpu.SMEM((spots, 3), jnp.int32), pltpu.VMEM((spots, NOTE, f), jnp.bfloat16)]
        + [pltpu.VMEM((spots, f, f), jnp.bfloat16)]
        + [pltpu.VMEM(ext, f32)] * 2 + [pltpu.VMEM(gp, f32)] * 2
        + [pltpu.SemaphoreType.DMA((15 + len(buffers),)), pltpu.SemaphoreType.DMA((spots,))]
        + [pltpu.VMEM(x.shape, x.dtype) for x in (probe, *tables)]
        + ([] if first else [pltpu.VMEM(ext, f32), pltpu.VMEM(gp, f32)])
        + [pltpu.VMEM((PAIR, 2, f, f), f32)] * 2 + [split] * 4,
        compiler_params=pltpu.CompilerParams(vmem_limit_bytes=60 << 20),
        cost_estimate=pl.CostEstimate(flops=4 * 10**9 * spots // 4, bytes_accessed=16 << 20, transcendentals=0),
    )(me, *buffers, *field, probe, *tables, *(grads or ()))


def from_neighbour(block, down, right):
    axes = ("col", "row")
    cols, rows = (lax.axis_size(axis) for axis in axes)
    route = []
    for c in range(cols):
        for r in range(rows):
            if 0 <= c + right < cols and 0 <= r + down < rows:
                route.append(((c + right) * rows + r + down, c * rows + r))
    return lax.ppermute(block, axes, route)


def with_edges(tile, west, east, h):
    top = jnp.concatenate([west[:, :h], tile[:, :h], east[:, :h]], axis=2)
    bottom = jnp.concatenate([west[:, -h:], tile[:, -h:], east[:, -h:]], axis=2)
    return tile, west, east, from_neighbour(bottom, -1, 0), from_neighbour(top, 1, 0)


def finish_kernel(middle, north, south, west, east, top, bottom, own, out_ref):
    height, width = middle.shape[1:]
    h = north.shape[1]
    rows, cols = pl.ds(h, height), slice(width - h, width)
    out_ref[0] = middle[0]
    out_ref[0, 0:h] += north[0]
    out_ref[0, height - h:height] += south[0]
    out_ref[0, :, 0:h] += west[0, rows]
    out_ref[0, :, cols] += east[0, rows]
    out_ref[0, 0:h, 0:h] += top[0, :, 0:h]
    out_ref[0, 0:h, cols] += top[0, :, h:]
    out_ref[0, height - h:height, 0:h] += bottom[0, :, 0:h]
    out_ref[0, height - h:height, cols] += bottom[0, :, h:]
    out_ref[0] = own[0] - step_size * out_ref[0]


def finish(*parts):
    blocks = [pl.BlockSpec((1,) + piece.shape[1:], lambda p: (p, 0, 0)) for piece in parts]
    return pl.pallas_call(
        finish_kernel,
        grid=(2,),
        out_shape=jax.ShapeDtypeStruct(parts[0].shape, jnp.float32),
        in_specs=blocks,
        out_specs=blocks[0],
        compiler_params=pltpu.CompilerParams(vmem_limit_bytes=60 << 20),
    )(*parts)


def on_device(object_field, probe_wave, amplitude, owners, row_offset, col_offset):
    frame_size = probe_wave.shape[1]
    half_frame = frame_size // 2
    acquired = amplitude.shape[0]
    axes = ("col", "row")
    col_count, row_count = lax.axis_size("col"), lax.axis_size("row")
    me = lax.axis_index("col").astype(jnp.int32)[None]
    capacity = 2 * acquired // col_count
    base = min(BASE, capacity)
    tables = transform_tables(frame_size)

    extra = capacity - base
    spares = acquired // capacity * extra
    everyone = col_count * row_count
    extra = capacity - base
    spares = acquired // capacity * extra
    count, *packed = pack(owners, row_offset, col_offset, amplitude, base, col_count, spares)
    main, spare = packed[:base], packed[base:]
    west = from_neighbour(object_field[:, :, -half_frame:], 0, -1)
    east = from_neighbour(object_field[:, :, :half_frame], 0, 1)
    west, east, main = lax.optimization_barrier((west, east, main))
    got = [lax.all_to_all(x, "col", 0, 0, tiled=True) for x in main]
    field = with_edges(object_field, west, east, half_frame)
    own, field = lax.optimization_barrier((own_terms(field), field))
    if spare:
        got.append(lax.all_gather(spare[0][:extra], "col", axis=0, tiled=True))
    grads = run_frames(me, got[:1], field, probe_wave, tables, None, False)
    *parts, probe_part = run_frames(me, got[1:], field, probe_wave, tables, grads, True)

    def exchange(west, east, north, south, middle, probe_part, own):
        from_west, from_east = from_neighbour(east, 0, -1), from_neighbour(west, 0, 1)
        from_north, from_south = from_neighbour(south, -1, 0), from_neighbour(north, 1, 0)
        pieces = probe_part.reshape(everyone, -1, probe_part.shape[-1])
        counts = jnp.broadcast_to(count.astype(jnp.float32), (everyone, 8, probe_part.shape[-1]))
        pieces = lax.all_to_all(jnp.concatenate([pieces, counts], axis=1), axes, 0, 0, tiled=True)
        most = jnp.max(pieces[:, -1, 0])
        piece = jnp.sum(pieces[:, :-8], axis=0) / math.sqrt(acquired * everyone)
        piece, from_west, from_east = lax.optimization_barrier((piece, from_west, from_east))
        up = jnp.concatenate([from_west[:, :half_frame], from_east[:, :half_frame]], axis=2)
        down = jnp.concatenate([from_west[:, -half_frame:], from_east[:, -half_frame:]], axis=2)
        top, bottom = from_neighbour(down, -1, 0), from_neighbour(up, 1, 0)
        whole = jnp.broadcast_to(piece[None], (everyone,) + piece.shape)
        whole = lax.all_to_all(whole, axes, 0, 0, tiled=True).reshape(probe_part.shape)
        return finish(middle, from_north, from_south, from_west, from_east, top, bottom, own), whole, most

    new_object, probe_gradient, most = exchange(*parts, probe_part, own)
    if not spare:
        return (new_object, probe_gradient)

    def the_rest(new_object, probe_gradient):
        def some(state):
            turn, *grads = state
            block = lax.dynamic_slice_in_dim(spare[0], turn * extra, extra, 0)
            block = lax.all_gather(block, "col", axis=0, tiled=True)
            return (turn + 1, *run_frames(me, [block], field, probe_wave, tables, grads, False))

        f, h = frame_size, half_frame
        height, width = object_field.shape[1:]
        zeros = (jnp.zeros((2, height + f, width + f)), jnp.zeros((2, 2, f + 8, h)))
        turn, grad, gp = lax.while_loop(
            lambda state: state[0] * extra < most.astype(jnp.int32), some, (jnp.ones((), jnp.int32), *zeros)
        )
        gp = jnp.concatenate([gp[:, 0], gp[:, 1]], axis=2)
        gp = gp[:, 8:].at[:, f - 8 :].add(gp[:, :8])
        rows, cols = slice(h, h + height), slice(h, h + width)
        parts = grad[:, :, :h], grad[:, :, h + width :], grad[:, :h, cols], grad[:, h + height :, cols], grad[:, rows, cols]
        new_object, added, _ = exchange(*parts, gp, new_object)
        return new_object, probe_gradient + added

    return lax.cond(
        most > extra, the_rest, lambda *results: results, new_object, probe_gradient
    )


def solution(mesh):
    in_specs = (
        P(None, "row", "col"),
        P(),
        P(("col", "row"), None, None),
        P(("col", "row"), None),
        P(("col", "row")),
        P(("col", "row")),
    )
    out_specs = (P(None, "row", "col"), P())
    return jax.shard_map(
        on_device, mesh=mesh, in_specs=in_specs, out_specs=out_specs, check_vma=False
    )
```

```python
import math

import jax
import jax.numpy as jnp
import numpy as np
from jax import lax
from jax.sharding import PartitionSpec as P
from jax.experimental import pallas as pl
from jax.experimental.pallas import tpu as pltpu


def transform_tables(length):
    half = length // 2
    n = np.arange(half)

    def table(k):
        angles = (n[:, None] * k[None, :]) % length * (2.0 * np.pi / length)
        c, s = np.cos(angles) / np.sqrt(length), np.sin(angles) / np.sqrt(length)
        return np.block([[c, -s], [s, c]]).astype(np.float32)

    def parts(m):
        high = m.astype(jnp.bfloat16)
        return high, (m - high.astype(np.float32)).astype(jnp.bfloat16)

    even, odd = table(2 * n), table(2 * n + 1)
    rights = [np.concatenate([h, l], 0) for h, l in map(parts, (even, odd, even.T, odd.T))]
    lefts = [np.concatenate([h, l], 1) for h, l in map(parts, (even.T, odd.T, even, odd))]
    pick = np.eye(length, dtype=np.float32)[np.concatenate([2 * n, 2 * n + 1])].astype(jnp.bfloat16)
    return jnp.asarray(np.stack(rights)), jnp.asarray(np.stack(lefts)), jnp.asarray(np.stack([pick, pick.T]))


def dot(a, b):
    return jnp.dot(a, b, preferred_element_type=jnp.float32)


def cat(parts, axis):
    return jnp.concatenate(parts, axis=axis)


def put(ref, where, x, rows, cols):
    high = x.astype(jnp.bfloat16)
    ref[where, 0, rows, cols] = high
    ref[where, 1, rows, cols] = (x - high.astype(jnp.float32)).astype(jnp.bfloat16)


def dot_right(ref, where, table):
    size = table.shape[1]
    high = ref[where, 0]
    return dot(cat([high, ref[where, 1], high], 1), cat([table[:size], table], 0))


def dot_left(table, ref, where):
    size = table.shape[0]
    high = ref[where, 0]
    return dot(cat([table[:, :size], table], 1), cat([high, ref[where, 1], high], 0))


CH = 16
PAIR = 4
step_size = 0.05
smooth_weight = 0.5
BASE = 2


def frames_step(places, slots, keep_all, frames_ref, ext_ref, right_ref, left_ref, pick_ref, grad_ref, probe_ref, gp_ref, wave_ref, prolled_ref, one_ref, two_ref, three_ref, four_ref):
    f = wave_ref.shape[2]
    h = f // 2
    count = len(places)
    each = range(count)
    halves = (slice(0, h), slice(h, f))
    lane = lax.broadcasted_iota(jnp.int32, (CH, h), 1)
    sub = lax.broadcasted_iota(jnp.int32, (8, f + h), 0)
    rr = [lax.rem(r, 8) for r, c in places]
    cc = [lax.rem(c, 128) for r, c in places]
    r8 = [pl.multiple_of(places[n][0] - rr[n], 8) for n in each]
    window = [pl.ds(pl.multiple_of(places[n][1] - cc[n], 128), f + h) for n in each]
    keep = [lane >= cc[n] for n in each]
    keep_rows = [sub >= rr[n] for n in each]

    def patch(n, p, i):
        w = ext_ref[p, pl.ds(pl.multiple_of(r8[n] + i, 8), CH), window[n]]
        if i == 0:
            w2 = ext_ref[p, pl.ds(pl.multiple_of(r8[n] + f, 8), 8), window[n]]
            w = cat([jnp.where(keep_rows[n], w[:8], w2), w[8:]], 0)
        return jnp.where(keep[n], w[:, :h], w[:, f:]), w[:, h:f]

    def probe(n, p, i):
        rows = pl.ds(8 - rr[n] + i, CH)
        y0 = pltpu.roll(probe_ref[p, 0, rows, :], cc[n], 1)
        y1 = pltpu.roll(probe_ref[p, 1, rows, :], cc[n], 1)
        return jnp.where(keep[n], y0, y1), jnp.where(keep[n], y1, y0)

    for n in each:
        for i in range(0, f, CH):
            rows = slice(i, i + CH)
            qr, qi, pr, pi = patch(n, 0, i), patch(n, 1, i), probe(n, 0, i), probe(n, 1, i)
            er, ei = [], []
            for t in range(2):
                prolled_ref[n, 0, rows, halves[t]] = pr[t]
                prolled_ref[n, 1, rows, halves[t]] = pi[t]
                er.append(pr[t] * qr[t] - pi[t] * qi[t])
                ei.append(pr[t] * qi[t] + pi[t] * qr[t])
                wave_ref[n, 0, rows, halves[t]] = er[t]
                wave_ref[n, 1, rows, halves[t]] = ei[t]
            put(one_ref.at[n], 0, er[0] + er[1], rows, halves[0])
            put(one_ref.at[n], 0, ei[0] + ei[1], rows, halves[1])
            put(one_ref.at[n], 1, er[0] - er[1], rows, halves[0])
            put(one_ref.at[n], 1, ei[0] - ei[1], rows, halves[1])
    for n in each:
        for w in range(2):
            y = dot_right(one_ref.at[n], w, right_ref[w])
            for i in range(0, h, CH):
                a, b = y[i:i + CH], y[h + i:h + i + CH]
                u, v = a + b, a - b
                put(two_ref.at[n], 0, u[:, :h], slice(i, i + CH), halves[w])
                put(two_ref.at[n], 0, u[:, h:], slice(h + i, h + i + CH), halves[w])
                put(two_ref.at[n], 1, v[:, :h], slice(i, i + CH), halves[w])
                put(two_ref.at[n], 1, v[:, h:], slice(h + i, h + i + CH), halves[w])
    for n in each:
        meas = dot(pick_ref[0], dot(frames_ref[slots[n]], pick_ref[1]).astype(jnp.bfloat16))
        for w in range(2):
            far = dot_left(left_ref[w], two_ref.at[n], w)
            for i in range(0, h, CH):
                xr, xi = far[i:i + CH], far[h + i:h + i + CH]
                s = meas[w * h + i:w * h + i + CH] * lax.rsqrt(jnp.maximum(xr * xr + xi * xi, 1.0))
                put(three_ref.at[n], w, xr * s, slice(i, i + CH), slice(0, f))
                put(three_ref.at[n], w, xi * s, slice(h + i, h + i + CH), slice(0, f))
    for n in each:
        be, bo = dot_left(left_ref[2], three_ref.at[n], 0), dot_left(left_ref[3], three_ref.at[n], 1)
        for i in range(0, h, CH):
            for part in range(2):
                j = part * h + i
                top, bot = be[j:j + CH] + bo[j:j + CH], be[j:j + CH] - bo[j:j + CH]
                for w in range(2):
                    put(four_ref.at[n], w, top[:, halves[w]], slice(i, i + CH), halves[part])
                    put(four_ref.at[n], w, bot[:, halves[w]], slice(h + i, h + i + CH), halves[part])
    for n in each:
        de, do = dot_right(four_ref.at[n], 0, right_ref[2]), dot_right(four_ref.at[n], 1, right_ref[3])
        fits = lane < 128 - cc[n]
        for i in range(0, f, CH):
            rows = slice(i, i + CH)
            a, b = de[rows], do[rows]
            lf, rt = a + b, a - b
            qr, qi = patch(n, 0, i), patch(n, 1, i)
            outs, back = [[], []], [[], []]
            for t, x in enumerate((lf, rt)):
                dr = wave_ref[n, 0, rows, halves[t]] - x[:, :h]
                di = wave_ref[n, 1, rows, halves[t]] - x[:, h:]
                if n:
                    dr, di = jnp.where(keep_all[n], dr, 0.0), jnp.where(keep_all[n], di, 0.0)
                pr, pi = prolled_ref[n, 0, rows, halves[t]], prolled_ref[n, 1, rows, halves[t]]
                outs[0].append(pr * dr + pi * di)
                outs[1].append(pr * di - pi * dr)
                back[0].append(qr[t] * dr + qi[t] * di)
                back[1].append(qr[t] * di - qi[t] * dr)
            for p in range(2):
                first = jnp.where(keep[n], outs[p][0], 0.0)
                full = cat([first, outs[p][1], outs[p][0] - first], 1)
                if i == 0:
                    head = jnp.where(keep_rows[n], full[:8], 0.0)
                    grad_ref[p, pl.ds(pl.multiple_of(r8[n] + f, 8), 8), window[n]] += full[:8] - head
                    full = cat([head, full[8:]], 0)
                grad_ref[p, pl.ds(pl.multiple_of(r8[n] + i, 8), CH), window[n]] += full
                y0 = pltpu.roll(back[p][0], lax.rem(128 - cc[n], 128), 1)
                y1 = pltpu.roll(back[p][1], lax.rem(128 - cc[n], 128), 1)
                spot = pl.ds(8 - rr[n] + i, CH)
                gp_ref[p, 0, spot, :] += jnp.where(fits, y0, y1)
                gp_ref[p, 1, spot, :] += jnp.where(fits, y1, y0)


NOTE = 16


def pack_kernel(base, owners_ref, rows_ref, cols_ref, amp_ref, count_ref, *rest):
    main, rest = rest[:base], rest[base:]
    spare, (seen_ref, note_ref, sems) = rest[:-3], rest[-3:]
    acquired, f = amp_ref.shape[:2]
    col_count = main[0].shape[0]
    lane = lax.broadcasted_iota(jnp.int32, (NOTE, amp_ref.shape[2]), 1)
    line = lax.broadcasted_iota(jnp.int32, (NOTE, amp_ref.shape[2]), 0)
    note_ref[...] = jnp.zeros_like(note_ref)

    @pl.loop(0, col_count)
    def _(n):
        seen_ref[n] = 0

    def place(k, spared):
        owner = owners_ref[k, 0]
        rank = seen_ref[owner]
        seen_ref[owner] = rank + 1
        words = (owner + 1, rows_ref[k] // 256, lax.rem(rows_ref[k], 256), cols_ref[k] // 256, lax.rem(cols_ref[k], 256))
        note = jnp.zeros(lane.shape, jnp.int32)
        for n, word in enumerate(words):
            note = jnp.where((lane == n) & (line == 0), word, note)
        spot = jnp.where(rank < base, owner * base + rank, col_count * base + spared)
        note_ref[spot] = note.astype(jnp.float32).astype(jnp.bfloat16)

        for n in range(base):
            @pl.when(rank == n)
            def _():
                pltpu.make_async_copy(amp_ref.at[k], main[n].at[owner, pl.ds(0, f)], sems.at[k]).start()

        if spare:
            @pl.when(rank >= base)
            def _():
                pltpu.make_async_copy(amp_ref.at[k], spare[0].at[spared, pl.ds(0, f)], sems.at[k]).start()

        return spared + jnp.where(rank >= base, 1, 0)

    spared = lax.fori_loop(0, acquired, place, 0)
    count_ref[0] = spared
    copies = []
    for n in range(note_ref.shape[0]):
        slot = main[n % base].at[n // base] if n < col_count * base else spare[0].at[n - col_count * base]
        copies.append(pltpu.make_async_copy(note_ref.at[n], slot.at[pl.ds(f, NOTE)], sems.at[acquired + n]))
    for copy in copies:
        copy.start()

    @pl.loop(0, acquired)
    def _(k):
        pltpu.make_async_copy(amp_ref.at[k], main[0].at[0, pl.ds(0, f)], sems.at[k]).wait()

    for copy in copies:
        copy.wait()


def pack(owners, row_offset, col_offset, amplitude, base, col_count, spares):
    frame = (amplitude.shape[1] + NOTE, amplitude.shape[2])
    smem, hbm = pl.BlockSpec(memory_space=pltpu.SMEM), pl.BlockSpec(memory_space=pl.ANY)
    shapes = [jax.ShapeDtypeStruct((1,), jnp.int32)]
    shapes += [jax.ShapeDtypeStruct((col_count,) + frame, amplitude.dtype)] * base
    if spares:
        shapes.append(jax.ShapeDtypeStruct((spares,) + frame, amplitude.dtype))
    notes = col_count * base + spares
    return pl.pallas_call(
        lambda *refs: pack_kernel(base, *refs),
        out_shape=shapes,
        in_specs=[smem] * 3 + [pl.BlockSpec(memory_space=pltpu.VMEM)],
        out_specs=[smem] + [hbm] * (len(shapes) - 1),
        scratch_shapes=[
            pltpu.SMEM((col_count,), jnp.int32),
            pltpu.VMEM((notes, NOTE, frame[1]), amplitude.dtype),
            pltpu.SemaphoreType.DMA((amplitude.shape[0] + notes,)),
        ],
    )(owners, row_offset, col_offset, amplitude)


def own_terms_kernel(x_ref, west_ref, east_ref, north_ref, south_ref, out_ref):
    x = x_ref[0]
    height, width = x.shape
    row = lax.broadcasted_iota(jnp.int32, x.shape, 0)
    col = lax.broadcasted_iota(jnp.int32, x.shape, 1)
    h = west_ref.shape[2]
    cols = slice(h, h + width)
    above = jnp.where(row == 0, north_ref[0, h - 1:h, cols], pltpu.roll(x, 1, 0))
    below = jnp.where(row == height - 1, south_ref[0, 0:1, cols], pltpu.roll(x, height - 1, 0))
    before = jnp.where(col == 0, west_ref[0, :, h - 1:h], pltpu.roll(x, 1, 1))
    after = jnp.where(col == width - 1, east_ref[0, :, 0:1], pltpu.roll(x, width - 1, 1))
    laplacian = 4.0 * x - above - below - before - after
    out_ref[0] = x - (step_size * smooth_weight) * laplacian


def own_terms(field):
    blocks = [pl.BlockSpec((1,) + piece.shape[1:], lambda p: (p, 0, 0)) for piece in field]
    return pl.pallas_call(
        own_terms_kernel,
        grid=(2,),
        out_shape=jax.ShapeDtypeStruct(field[0].shape, jnp.float32),
        in_specs=blocks,
        out_specs=blocks[0],
        compiler_params=pltpu.CompilerParams(vmem_limit_bytes=60 << 20),
    )(*field)


def frames_kernel(layout, first, last, me_ref, *refs):
    refs = list(refs)
    take = lambda n: [refs.pop(0) for _ in range(n)]
    buffers = take(len(layout))
    pieces = take(5)
    constants = take(4)
    grads_in = take(0 if first else 2)
    outs = take(6 if last else 2)
    list_ref, note_ref, frames_ref, ext_ref, grad_ref, probe_ref, gp_ref, sems, frame_sems = take(9)
    probe_in, right_ref, left_ref, pick_ref = held = take(4)
    f = probe_in.shape[1]
    h = f // 2
    height, width = pieces[0].shape[1:]
    every = slice(None)
    areas = (
        (every, pl.ds(h, height), pl.ds(h, width)),
        (every, pl.ds(h, height), pl.ds(0, h)),
        (every, pl.ds(h, height), pl.ds(h + width, h)),
        (every, pl.ds(0, h)),
        (every, pl.ds(h + height, h)),
    )
    copies = [pltpu.make_async_copy(piece, ext_ref.at[area], sems.at[n]) for n, (piece, area) in enumerate(zip(pieces, areas))]
    late = [pltpu.make_async_copy(constants[n], held[n], sems.at[9 + n]) for n in range(4)]
    if not first:
        carried = [
            pltpu.make_async_copy(grads_in[0], grad_ref, sems.at[13]),
            pltpu.make_async_copy(grads_in[1], gp_ref, sems.at[14]),
        ]
    if not first:
        late += carried
    for copy in copies + late:
        copy.start()
    scratch = refs
    notes = [
        pltpu.make_async_copy(
            buffers[b].at[pl.ds(0, len(slots)), pl.ds(f, NOTE)],
            note_ref.at[pl.ds(sum(len(x) for x in layout[:b]), len(slots))],
            sems.at[15 + b],
        )
        for b, slots in enumerate(layout)
    ]
    for copy in notes:
        copy.start()
    for copy in notes:
        copy.wait()
    lane = lax.broadcasted_iota(jnp.int32, (NOTE, note_ref.shape[2]), 1)
    row_scale = jnp.where(lane == 0, 65536.0, jnp.where(lane == 1, 256.0, jnp.where(lane == 2, 1.0, 0.0)))
    col_scale = jnp.where(lane == 3, 256.0, jnp.where(lane == 4, 1.0, 0.0))
    found = []
    for spot in range(note_ref.shape[0]):
        note = note_ref[spot].astype(jnp.float32)
        found.append((jnp.sum(note * row_scale).astype(jnp.int32), jnp.sum(note * col_scale).astype(jnp.int32)))
    total = 0
    for b, slots in enumerate(layout):
        for n, slot in enumerate(slots):
            spot = sum(len(x) for x in layout[:b]) + n
            row, col = found[spot]
            used = row // 65536 == me_ref[0] + 1

            @pl.when(used)
            def _():
                list_ref[total, 0] = lax.rem(row, 65536)
                list_ref[total, 1] = col
                list_ref[total, 2] = spot
                pltpu.make_async_copy(buffers[b].at[n, pl.ds(0, f)], frames_ref.at[spot], frame_sems.at[spot]).start()

            total = total + jnp.where(used, 1, 0)
    if first:
        gp_ref[...] = jnp.zeros_like(gp_ref)
        grad_ref[...] = jnp.zeros_like(grad_ref)
    for copy in copies:
        copy.wait()
    for copy in late:
        copy.wait()
    for p in range(2):
        for t in range(2):
            cols = slice(t * h, t * h + h)
            probe_ref[p, t, 0:8, :] = probe_in[p, f - 8:f, cols]
            probe_ref[p, t, 8:8 + f, :] = probe_in[p, :, cols]

    @pl.loop(0, total)
    def _(k):
        spot = list_ref[k, 2]
        pltpu.make_async_copy(buffers[0].at[0, pl.ds(0, f)], frames_ref.at[spot], frame_sems.at[spot]).wait()

    @pl.loop(0, (total + PAIR - 1) // PAIR)
    def _(k):
        places, spots = [], []
        for n in range(PAIR):
            item = jnp.minimum(k * PAIR + n, total - 1)
            places.append((list_ref[item, 0], list_ref[item, 1]))
            spots.append(list_ref[item, 2])
        frames_step(places, spots, [k * PAIR + n < total for n in range(PAIR)], frames_ref, ext_ref, right_ref, left_ref, pick_ref, grad_ref, probe_ref, gp_ref, *scratch)

    if not last:
        ends = [(grad_ref, outs[0]), (gp_ref, outs[1])]
    else:
        spots = [
            (every, every, pl.ds(0, h)),
            (every, every, pl.ds(h + width, h)),
            (every, pl.ds(0, h), pl.ds(h, width)),
            (every, pl.ds(h + height, h), pl.ds(h, width)),
            areas[0],
        ]
        ends = [(grad_ref.at[spot], outs[n]) for n, spot in enumerate(spots)]
        pieces_ref = outs[5]
        devices, tall = pieces_ref.shape[0], pieces_ref.shape[1] - 8
        gp_ref[:, :, f:f + 8, :] += gp_ref[:, :, 0:8, :]
        pieces_ref[:, tall:, :] = jnp.full((devices, 8, f), me_ref[1].astype(jnp.float32))
        for n in range(devices):
            p, first_row = n * tall // f, n * tall % f + 8
            for t in range(2):
                pieces_ref[n, 0:tall, t * h:t * h + h] = gp_ref[p, t, first_row:first_row + tall, :]
    ends = [pltpu.make_async_copy(a, b, sems.at[n]) for n, (a, b) in enumerate(ends)]
    for copy in ends:
        copy.start()
    for copy in ends:
        copy.wait()


def run_frames(me, buffers, field, probe, tables, grads, devices):
    layout = [list(range(buffer.shape[0])) for buffer in buffers]
    last = devices is not None
    f = probe.shape[1]
    h = f // 2
    height, width = field[0].shape[1:]
    first = grads is None
    vm, hbm, smem = (pl.BlockSpec(memory_space=m) for m in (pltpu.VMEM, pl.ANY, pltpu.SMEM))
    f32 = jnp.float32
    ext, gp = (2, height + f, width + f), (2, 2, f + 8, h)
    if last:
        shapes = [(2, height + f, h)] * 2 + [(2, h, width)] * 2 + [(2, height, width), (devices, 2 * f // devices + 8, f)]
        out_specs = [hbm] * 5 + [vm]
    else:
        shapes, out_specs = [ext, gp], [hbm] * 2
    spots = sum(len(x) for x in layout)
    split = pltpu.VMEM((PAIR, 2, 2, f, f), jnp.bfloat16)
    return pl.pallas_call(
        lambda *refs: frames_kernel(layout, first, last, *refs),
        out_shape=[jax.ShapeDtypeStruct(x, f32) for x in shapes],
        in_specs=[smem] + [hbm] * (len(buffers) + 9 + (0 if first else 2)),
        out_specs=out_specs,
        scratch_shapes=[pltpu.SMEM((spots, 3), jnp.int32), pltpu.VMEM((spots, NOTE, f), jnp.bfloat16)]
        + [pltpu.VMEM((spots, f, f), jnp.bfloat16)]
        + [pltpu.VMEM(ext, f32)] * 2 + [pltpu.VMEM(gp, f32)] * 2
        + [pltpu.SemaphoreType.DMA((15 + len(buffers),)), pltpu.SemaphoreType.DMA((spots,))]
        + [pltpu.VMEM(x.shape, x.dtype) for x in (probe, *tables)]
        + [pltpu.VMEM((PAIR, 2, f, f), f32)] * 2 + [split] * 4,
        compiler_params=pltpu.CompilerParams(vmem_limit_bytes=60 << 20),
        cost_estimate=pl.CostEstimate(flops=4 * 10**9 * spots // 4, bytes_accessed=16 << 20, transcendentals=0),
    )(me, *buffers, *field, probe, *tables, *(grads or ()))


def from_neighbour(block, down, right):
    axes = ("col", "row")
    cols, rows = (lax.axis_size(axis) for axis in axes)
    route = []
    for c in range(cols):
        for r in range(rows):
            if 0 <= c + right < cols and 0 <= r + down < rows:
                route.append(((c + right) * rows + r + down, c * rows + r))
    return lax.ppermute(block, axes, route)


def with_edges(tile, west, east, h):
    top = jnp.concatenate([west[:, :h], tile[:, :h], east[:, :h]], axis=2)
    bottom = jnp.concatenate([west[:, -h:], tile[:, -h:], east[:, -h:]], axis=2)
    return tile, west, east, from_neighbour(bottom, -1, 0), from_neighbour(top, 1, 0)


def finish_kernel(middle, north, south, west, east, top, bottom, own, out_ref):
    height, width = middle.shape[1:]
    h = north.shape[1]
    rows, cols = pl.ds(h, height), slice(width - h, width)
    out_ref[0] = middle[0]
    out_ref[0, 0:h] += north[0]
    out_ref[0, height - h:height] += south[0]
    out_ref[0, :, 0:h] += west[0, rows]
    out_ref[0, :, cols] += east[0, rows]
    out_ref[0, 0:h, 0:h] += top[0, :, 0:h]
    out_ref[0, 0:h, cols] += top[0, :, h:]
    out_ref[0, height - h:height, 0:h] += bottom[0, :, 0:h]
    out_ref[0, height - h:height, cols] += bottom[0, :, h:]
    out_ref[0] = own[0] - step_size * out_ref[0]


def finish(*parts):
    blocks = [pl.BlockSpec((1,) + piece.shape[1:], lambda p: (p, 0, 0)) for piece in parts]
    return pl.pallas_call(
        finish_kernel,
        grid=(2,),
        out_shape=jax.ShapeDtypeStruct(parts[0].shape, jnp.float32),
        in_specs=blocks,
        out_specs=blocks[0],
        compiler_params=pltpu.CompilerParams(vmem_limit_bytes=60 << 20),
    )(*parts)


def on_device(object_field, probe_wave, amplitude, owners, row_offset, col_offset):
    frame_size = probe_wave.shape[1]
    half_frame = frame_size // 2
    acquired = amplitude.shape[0]
    axes = ("col", "row")
    col_count, row_count = lax.axis_size("col"), lax.axis_size("row")
    me = lax.axis_index("col").astype(jnp.int32)[None]
    capacity = 2 * acquired // col_count
    base = min(BASE, capacity)
    tables = transform_tables(frame_size)

    extra = capacity - base
    spares = acquired // capacity * extra
    everyone = col_count * row_count
    extra = capacity - base
    spares = acquired // capacity * extra
    count, *packed = pack(owners, row_offset, col_offset, amplitude, base, col_count, spares)
    main, spare = packed[:base], packed[base:]
    west = from_neighbour(object_field[:, :, -half_frame:], 0, -1)
    east = from_neighbour(object_field[:, :, :half_frame], 0, 1)
    west, east, main = lax.optimization_barrier((west, east, main))
    got = [lax.all_to_all(main[0], "col", 0, 0, tiled=True)]
    field = with_edges(object_field, west, east, half_frame)
    own, field = lax.optimization_barrier((own_terms(field), field))
    if spare:
        more = lax.all_gather(spare[0][:extra], "col", axis=0, tiled=True)
        more, main = lax.optimization_barrier((more, main))
        got.append(more)
    grads = run_frames(me, got, field, probe_wave, tables, None, None)
    got = [lax.all_to_all(x, "col", 0, 0, tiled=True) for x in main[1:]]
    parts = run_frames(jnp.concatenate([me, count]), got, field, probe_wave, tables, grads, everyone)

    def exchange(west, east, north, south, middle, pieces, own):
        from_west, from_east = from_neighbour(east, 0, -1), from_neighbour(west, 0, 1)
        from_north, from_south = from_neighbour(south, -1, 0), from_neighbour(north, 1, 0)
        pieces = lax.all_to_all(pieces, axes, 0, 0, tiled=True)
        most = jnp.max(pieces[:, -1, 0])
        piece = jnp.sum(pieces[:, :-8], axis=0) / math.sqrt(acquired * everyone)
        piece, from_north, from_south = lax.optimization_barrier((piece, from_north, from_south))
        up = jnp.concatenate([from_west[:, :half_frame], from_east[:, :half_frame]], axis=2)
        down = jnp.concatenate([from_west[:, -half_frame:], from_east[:, -half_frame:]], axis=2)
        top, bottom = from_neighbour(down, -1, 0), from_neighbour(up, 1, 0)
        whole = jnp.broadcast_to(piece[None], (everyone,) + piece.shape)
        whole = lax.all_to_all(whole, axes, 0, 0, tiled=True).reshape(probe_wave.shape)
        return finish(middle, from_north, from_south, from_west, from_east, top, bottom, own), whole, most

    new_object, probe_gradient, most = exchange(*parts, own)
    if not spare:
        return (new_object, probe_gradient)

    def the_rest(new_object, probe_gradient):
        def some(state):
            turn, *grads = state
            block = lax.dynamic_slice_in_dim(spare[0], turn * extra, extra, 0)
            block = lax.all_gather(block, "col", axis=0, tiled=True)
            return (turn + 1, *run_frames(me, [block], field, probe_wave, tables, grads, None))

        f, h = frame_size, half_frame
        height, width = object_field.shape[1:]
        zeros = (jnp.zeros((2, height + f, width + f)), jnp.zeros((2, 2, f + 8, h)))
        turn, grad, gp = lax.while_loop(
            lambda state: state[0] * extra < most.astype(jnp.int32), some, (jnp.ones((), jnp.int32), *zeros)
        )
        gp = jnp.concatenate([gp[:, 0], gp[:, 1]], axis=2)
        gp = gp[:, 8:].at[:, f - 8 :].add(gp[:, :8]).reshape(everyone, -1, f)
        gp = jnp.concatenate([gp, jnp.zeros((everyone, 8, f))], axis=1)
        rows, cols = slice(h, h + height), slice(h, h + width)
        parts = grad[:, :, :h], grad[:, :, h + width :], grad[:, :h, cols], grad[:, h + height :, cols], grad[:, rows, cols]
        new_object, added, _ = exchange(*parts, gp, new_object)
        return new_object, probe_gradient + added

    return lax.cond(
        most > extra, the_rest, lambda *results: results, new_object, probe_gradient
    )


def solution(mesh):
    in_specs = (
        P(None, "row", "col"),
        P(),
        P(("col", "row"), None, None),
        P(("col", "row"), None),
        P(("col", "row")),
        P(("col", "row")),
    )
    out_specs = (P(None, "row", "col"), P())
    return jax.shard_map(
        on_device, mesh=mesh, in_specs=in_specs, out_specs=out_specs, check_vma=False
    )
```
